128 devices in a mesh: rows: 32 (over z, y, core), group: 4 (over x).
Axes of the slice: x: 4, y: 4, z: 4, core: 2. Of those that a mesh axis runs over, the one named last changes fastest.
Arguments:
- slab: float32 [786432, 512], P(('rows', 'group')), may hold values from -16 to 16
Outputs:
- updated: float32 [786432, 512], P(('rows', 'group'))
The draws below stay inside these ranges and needn't reach their ends.
All inputs are finite; a program needn't handle non-finite values.
Results may differ from the reference program's by a relative error of at most 0.0001.
Values sent between devices are 32-bit elements; how exact they have to be, the bound alone decides.
A program may use at most 128 MiB of HBM per device.

```python
import math
import jax
import jax.numpy as jnp
from jax import lax

COLS = 512
ROWS_DEV = 6144
ROWS = 786432
N_ROWS = 32
N_GROUP = 4


def draw_slab(key, part):
    key = jax.random.fold_in(key, 11)
    keys = jax.random.split(key, 3)
    base = jnp.clip(jax.random.normal(keys[0], (ROWS, COLS + 3), jnp.float32), -4.0, 4.0)
    mixed = base[:, 3:] + 0.6 * base[:, 2:-1] - 0.45 * base[:, :-3]
    column = jnp.exp(jax.random.uniform(keys[1], (COLS,), jnp.float32, math.log(0.1), 0.0))
    place = jnp.arange(ROWS, dtype=jnp.float32) / ROWS
    ramp = jnp.exp(0.5 * math.log(3.0) * place)
    rough = jnp.exp(jax.random.uniform(keys[2], (ROWS,), jnp.float32, 0.0, 0.5 * math.log(10.0)))
    values = mixed * column[None, :] * (ramp * rough)[:, None] / 3.3
    return values


def setup_inputs(seed: int = 0) -> dict:
    arg_keys = jax.random.split(jax.random.key(seed), 2)
    return {
        "slab": draw_slab(jax.random.fold_in(arg_keys[1], 71), 0),
    }


lower_bound = 0.1
spread_d = (4.0 * (1.0 - lower_bound ** 2) / lower_bound ** 4) ** (1.0 / 3.0)
weight_alpha = math.sqrt(1.0 + spread_d) + 0.5 * math.sqrt(8.0 - 4.0 * spread_d + 8.0 * (2.0 - lower_bound ** 2) / (lower_bound ** 2 * math.sqrt(1.0 + spread_d)))
weight_beta = (weight_alpha - 1.0) ** 2 / 4.0
weight_gamma = weight_alpha + weight_beta - 1.0

def block_gram(total, block):
    part = lax.dot_general(block.astype(jnp.float32), block.astype(jnp.float32), (((0,), (0,)), ((), ())), precision=lax.Precision.HIGHEST, preferred_element_type=jnp.float32)
    return (total + part, None)

def reference(slab):
    blocks = slab.reshape(N_ROWS * N_GROUP, ROWS_DEV, COLS)
    start = jnp.zeros((COLS, COLS), jnp.float32)
    gram, unused = lax.scan(block_gram, start, blocks)
    identity = jnp.eye(COLS, dtype=jnp.float32)
    shifted = weight_gamma / ROWS * gram + identity
    lower = jnp.linalg.cholesky(shifted)
    inverse_low = lax.linalg.triangular_solve(lower, identity, left_side=True, lower=True)
    inverse = lax.dot_general(inverse_low.astype(jnp.float32), inverse_low.astype(jnp.float32), (((0,), (0,)), ((), ())), precision=lax.Precision.HIGHEST, preferred_element_type=jnp.float32)
    mixing = weight_beta / weight_gamma * identity + (weight_alpha - weight_beta / weight_gamma) * inverse
    return jnp.dot(slab.astype(jnp.float32), mixing.astype(jnp.float32), precision=lax.Precision.HIGHEST, preferred_element_type=jnp.float32)
```

```python
import functools
import math

import jax
import jax.numpy as jnp
from jax import lax
from jax.experimental import pallas as pl
from jax.experimental.pallas import tpu as pltpu
from jax.sharding import PartitionSpec as P

lower_bound = 0.1
spread_d = (4.0 * (1.0 - lower_bound**2) / lower_bound**4) ** (1.0 / 3.0)
weight_alpha = math.sqrt(1.0 + spread_d) + 0.5 * math.sqrt(
    8.0
    - 4.0 * spread_d
    + 8.0 * (2.0 - lower_bound**2) / (lower_bound**2 * math.sqrt(1.0 + spread_d))
)
weight_beta = (weight_alpha - 1.0) ** 2 / 4.0
weight_gamma = weight_alpha + weight_beta - 1.0

MESH = pl.DeviceIdType.MESH
SIDE = 4
PLANE = SIDE * SIDE
BLOCK = 128
TILE = 8
CHUNK = 512
BLOCKS = [
    (0, 0), (0, 1), (0, 2), (0, 3), (1, 1),
    (1, 2), (1, 3), (2, 2), (2, 3), (3, 3),
]
HALF = 5 * BLOCK // TILE
STREAMS = [("xy", "z", 2, 0), ("yz", "x", 2, 32), ("zx", "y", 1, 64)]
VMEM_BYTES = 56 * 2**20
SHIFTS = [(i, j) for i in range(SIDE) for j in range(SIDE) if i or j]
GOOD = 8e-3

f32, bf16 = jnp.float32, jnp.bfloat16


def dot(left, right):
    return jnp.dot(left, right, preferred_element_type=f32)


def cross(left, right):
    return lax.dot_general(left, right, (((0,), (0,)), ((), ())), preferred_element_type=f32)


def split(value):
    high = value.astype(bf16)
    return high, (value - high.astype(f32)).astype(bf16)


def dot_three(left, right):
    left_high, left_low = split(left)
    right_high, right_low = split(right)
    return dot(left_high, right_high) + (dot(left_high, right_low) + dot(left_low, right_high))


def gram_kernel(
    slab, out, held, partial, packed, core_in, rs_a, rs_b, rs_c, ln_a, ln_b, ln_c, mine_a, mine_b,
    mine_c, full, load_sem, core_sem, rs_send, rs_recv, ln_send, ln_recv, ag_send, ag_recv,
):
    rows = slab.shape[0]
    index = lax.axis_index("rows")
    core = lax.rem(index, 2)
    here = {
        "x": lax.axis_index("group"),
        "y": lax.rem(lax.div(index, 2), SIDE),
        "z": lax.div(index, 2 * SIDE),
    }

    def device(shift):
        at = {name: lax.rem(here[name] + shift.get(name, 0), SIDE) for name in here}
        return ((at["z"] * SIDE + at["y"]) * 2 + core, at["x"])

    sibling = (index + 1 - 2 * core, here["x"])

    def load(i):
        part = pl.ds(i * CHUNK, CHUNK)
        return pltpu.make_async_copy(slab.at[part], held.at[part], load_sem.at[i])

    for i in range(rows // CHUNK):
        load(i).start()

    barrier = pltpu.get_barrier_semaphore()
    shifts = []
    for plane, _, _, _ in STREAMS:
        for i, j in SHIFTS:
            shift = {plane[0]: i, plane[1]: j}
            shift = tuple((name, shift[name]) for name in "xyz" if shift.get(name, 0))
            if shift not in shifts:
                shifts.append(shift)
    for shift in shifts:
        pl.semaphore_signal(barrier, inc=1, device_id=device(dict(shift)), device_id_type=MESH)
    pl.semaphore_signal(barrier, inc=1, device_id=sibling, device_id_type=MESH)

    for i in range(rows // CHUNK):
        load(i).wait()
        block = held[pl.ds(i * CHUNK, CHUNK), :]
        high = block.astype(bf16)
        low = ((block - high.astype(f32)) * 2.0).astype(bf16)
        term = cross(jnp.concatenate([high, high], 0), jnp.concatenate([high, low], 0))
        partial[...] = term if i == 0 else partial[...] + term

    for n, (i, j) in enumerate(BLOCKS):
        a = partial[i * BLOCK : (i + 1) * BLOCK, j * BLOCK : (j + 1) * BLOCK]
        b = partial[j * BLOCK : (j + 1) * BLOCK, i * BLOCK : (i + 1) * BLOCK]
        packed[n // 5, pl.ds((n % 5) * PLANE, PLANE)] = (a + b.T).reshape(PLANE, TILE, BLOCK)

    pl.semaphore_wait(barrier, len(shifts) + 1)

    give = pltpu.make_async_remote_copy(
        src_ref=packed.at[1 - core], dst_ref=core_in, send_sem=core_sem.at[0],
        recv_sem=core_sem.at[1], device_id=sibling, device_id_type=MESH,
    )
    give.start()
    give.wait()
    packed[core] = packed[core] + core_in[...]

    rs, ln, mine = (rs_a, rs_b, rs_c), (ln_a, ln_b, ln_c), (mine_a, mine_b, mine_c)
    spots = [here[plane[0]] * SIDE + here[plane[1]] for plane, _, _, _ in STREAMS]

    for s, (plane, _, units, first) in enumerate(STREAMS):
        for k, (i, j) in enumerate(SHIFTS):
            spot = lax.rem(here[plane[0]] + i, SIDE) * SIDE + lax.rem(here[plane[1]] + j, SIDE)
            pltpu.make_async_remote_copy(
                src_ref=packed.at[core, pl.ds(first + units * spot, units)], dst_ref=rs[s].at[k],
                send_sem=rs_send.at[s], recv_sem=rs_recv.at[s],
                device_id=device({plane[0]: i, plane[1]: j}), device_id_type=MESH,
            ).start()
    for s, (plane, line, units, first) in enumerate(STREAMS):
        pltpu.make_async_copy(rs[s], rs[s], rs_recv.at[s]).wait()
        mine[s][...] = packed[core, pl.ds(first + units * spots[s], units)] + jnp.sum(rs[s][...], axis=0)
        for k in range(SIDE - 1):
            pltpu.make_async_remote_copy(
                src_ref=mine[s], dst_ref=ln[s].at[k], send_sem=ln_send.at[s],
                recv_sem=ln_recv.at[s], device_id=device({line: k + 1}), device_id_type=MESH,
            ).start()
    for s, (plane, line, units, first) in enumerate(STREAMS):
        pltpu.make_async_copy(ln[s], ln[s], ln_recv.at[s]).wait()
        place = full.at[core, pl.ds(first + units * spots[s], units)]
        place[...] = mine[s][...] + jnp.sum(ln[s][...], axis=0)
        for i, j in SHIFTS:
            pltpu.make_async_remote_copy(
                src_ref=place, dst_ref=place, send_sem=ag_send.at[s], recv_sem=ag_recv.at[s],
                device_id=device({plane[0]: i, plane[1]: j}), device_id_type=MESH,
            ).start()
    for s, (plane, line, units, first) in enumerate(STREAMS):
        got = full.at[core, pl.ds(first, (PLANE - 1) * units)]
        pltpu.make_async_copy(got, got, ag_recv.at[s]).wait()
    back = pltpu.make_async_remote_copy(
        src_ref=full.at[core], dst_ref=full.at[core], send_sem=core_sem.at[2],
        recv_sem=core_sem.at[3], device_id=sibling, device_id_type=MESH,
    )
    back.start()
    for s, (plane, line, units, first) in enumerate(STREAMS):
        sent = full.at[core, pl.ds(first, (PLANE - 1) * units)]
        pltpu.make_async_copy(rs[s], rs[s], rs_send.at[s]).wait()
        pltpu.make_async_copy(ln[s], ln[s], ln_send.at[s]).wait()
        pltpu.make_async_copy(sent, sent, ag_send.at[s]).wait()
    back.wait()
    out[...] = full[...]


def reduced_gram(slab):
    rows, width = slab.shape
    unit = lambda *lead: pltpu.VMEM((*lead, TILE, BLOCK), f32)
    dma = pltpu.SemaphoreType.DMA
    return pl.pallas_call(
        gram_kernel,
        out_shape=jax.ShapeDtypeStruct((2, HALF, TILE, BLOCK), f32),
        in_specs=[pl.BlockSpec(memory_space=pl.ANY)],
        out_specs=pl.BlockSpec(memory_space=pltpu.VMEM),
        scratch_shapes=[
            pltpu.VMEM((rows, width), f32),
            pltpu.VMEM((width, width), f32),
            unit(2, HALF),
            unit(HALF),
            *[unit(PLANE - 1, units) for _, _, units, _ in STREAMS],
            *[unit(SIDE - 1, units) for _, _, units, _ in STREAMS],
            *[unit(units) for _, _, units, _ in STREAMS],
            unit(2, HALF),
            dma((rows // CHUNK,)),
            dma((4,)),
            *[dma((3,)) for _ in range(6)],
        ],
        compiler_params=pltpu.CompilerParams(
            collective_id=0, has_side_effects=True, vmem_limit_bytes=VMEM_BYTES
        ),
    )(slab)


def apply_kernel(
    scale, gram, slab, out, held, ready, shifted, work, mixing, load_sem, store_sem
):
    rows, width = slab.shape

    def load(i):
        part = pl.ds(i * CHUNK, CHUNK)
        return pltpu.make_async_copy(slab.at[part], held.at[part], load_sem.at[i])

    def store(i):
        part = pl.ds(i * CHUNK, CHUNK)
        return pltpu.make_async_copy(ready.at[part], out.at[part], store_sem.at[i])

    for i in range(rows // CHUNK):
        load(i).start()

    row_ids = lax.broadcasted_iota(jnp.int32, (width, width), 0)
    col_ids = lax.broadcasted_iota(jnp.int32, (width, width), 1)
    identity = (row_ids == col_ids).astype(f32)
    for n, (i, j) in enumerate(BLOCKS):
        a = gram[n // 5, pl.ds((n % 5) * PLANE, PLANE)].reshape(BLOCK, BLOCK)
        shifted[i * BLOCK : (i + 1) * BLOCK, j * BLOCK : (j + 1) * BLOCK] = a
        if i != j:
            shifted[j * BLOCK : (j + 1) * BLOCK, i * BLOCK : (i + 1) * BLOCK] = a.T
    matrix = shifted[...] * scale + identity

    diagonal = matrix * identity
    diagonal_row = jnp.sum(diagonal, axis=0, keepdims=True)
    diagonal_col = jnp.sum(diagonal, axis=1, keepdims=True)
    by_row, by_col = lax.rsqrt(diagonal_row), lax.rsqrt(diagonal_col)
    matrix = matrix * by_row * by_col
    shifted[...] = matrix
    low = 1.0 / jnp.max(diagonal_row, axis=1, keepdims=True)
    sums = jnp.sum(jnp.abs(matrix), axis=0, keepdims=True)
    high = jnp.maximum(jnp.max(sums, axis=1, keepdims=True), 1.0) * 1.01

    gap = 1.0 / (high - low)
    t_one = (high + low) * gap
    t_two = 2.0 * t_one * t_one - 1.0
    first = (t_one * identity) - (2.0 * gap) * matrix
    first_16 = first.astype(bf16)
    work[:width, :] = 2.0 * dot(first_16, first_16) - identity
    work[width:, :] = (4.0 * t_one / (t_two * (high + low))) * (t_one * identity + first)

    def more(carry):
        t, n = carry
        return jnp.logical_and(t[0, 0] < 8.0, n < 12)

    def double(carry):
        t, n = carry
        t_next = 2.0 * t * t - 1.0
        both = work[...]
        both_16 = both.astype(bf16)
        product = dot(both_16, both_16[:width])
        work[:width, :] = 2.0 * product[:width] - identity
        work[width:, :] = (2.0 * t / t_next) * (t * both[width:] + product[width:])
        return t_next, n + 1

    lax.while_loop(more, double, (t_two, 0))

    def unfinished(carry):
        size, n = carry
        return jnp.logical_and(size > GOOD * GOOD, n < 6)

    def refine(carry):
        _, n = carry
        inverse = work[width:, :]
        residual = identity - dot_three(shifted[...], inverse)
        work[width:, :] = inverse + dot(inverse.astype(bf16), residual.astype(bf16))
        return jnp.sum(residual * residual), n + 1

    size, _ = lax.while_loop(unfinished, refine, (jnp.float32(1e9), 0))

    @pl.when(jnp.logical_not(size <= GOOD * GOOD))
    def _():
        work[width:, :] = shifted[...]

        def eliminate(k, carry):
            value = work[width:, :]
            row = work[pl.ds(width + k, 1), :]
            at_col = col_ids == k
            col = jnp.sum(jnp.where(at_col, value, 0.0), axis=1, keepdims=True)
            pivot = 1.0 / jnp.sum(jnp.where(at_col[:1], row, 0.0), axis=1, keepdims=True)
            row = jnp.where(at_col[:1], pivot, row * pivot)
            value = jnp.where(at_col, 0.0, value) - col * row
            work[width:, :] = jnp.where(row_ids == k, row, value)
            return carry

        lax.fori_loop(0, width, eliminate, 0)

    inverse = work[width:, :]
    mixing[...] = (
        weight_beta / weight_gamma * identity
        + (weight_alpha - weight_beta / weight_gamma) * (inverse * by_row * by_col)
    )
    mixing_high, mixing_low = split(mixing[...])

    for i in range(rows // CHUNK):
        load(i).wait()
        part = pl.ds(i * CHUNK, CHUNK)
        high_part, low_part = split(held[part, :])
        ready[part, :] = dot(high_part, mixing_high) + (
            dot(high_part, mixing_low) + dot(low_part, mixing_high)
        )
        store(i).start()
    for i in range(rows // CHUNK):
        store(i).wait()


def applied(scale, gram, slab):
    rows, width = slab.shape
    dma = pltpu.SemaphoreType.DMA
    return pl.pallas_call(
        functools.partial(apply_kernel, scale),
        out_shape=jax.ShapeDtypeStruct((rows, width), f32),
        in_specs=[pl.BlockSpec(memory_space=pltpu.VMEM), pl.BlockSpec(memory_space=pl.ANY)],
        out_specs=pl.BlockSpec(memory_space=pl.ANY),
        scratch_shapes=[
            pltpu.VMEM((rows, width), f32),
            pltpu.VMEM((rows, width), f32),
            pltpu.VMEM((width, width), f32),
            pltpu.VMEM((2 * width, width), f32),
            pltpu.VMEM((width, width), f32),
            dma((rows // CHUNK,)),
            dma((rows // CHUNK,)),
        ],
        compiler_params=pltpu.CompilerParams(vmem_limit_bytes=VMEM_BYTES),
    )(gram, slab)


def local(slab):
    devices_all = lax.axis_size("rows") * lax.axis_size("group")
    scale = 0.5 * weight_gamma / (slab.shape[0] * devices_all)
    return applied(scale, reduced_gram(slab), slab)


def solution(mesh):
    placed = (P(("rows", "group"), None),)
    return jax.shard_map(
        local, mesh=mesh, in_specs=placed, out_specs=P(("rows", "group"), None), check_vma=False
    )
```

```python
import functools
import math

import jax
import jax.numpy as jnp
from jax import lax
from jax.experimental import pallas as pl
from jax.experimental.pallas import tpu as pltpu
from jax.sharding import PartitionSpec as P

lower_bound = 0.1
spread_d = (4.0 * (1.0 - lower_bound**2) / lower_bound**4) ** (1.0 / 3.0)
weight_alpha = math.sqrt(1.0 + spread_d) + 0.5 * math.sqrt(
    8.0
    - 4.0 * spread_d
    + 8.0 * (2.0 - lower_bound**2) / (lower_bound**2 * math.sqrt(1.0 + spread_d))
)
weight_beta = (weight_alpha - 1.0) ** 2 / 4.0
weight_gamma = weight_alpha + weight_beta - 1.0

MESH = pl.DeviceIdType.MESH
SIDE = 4
PLANE = SIDE * SIDE
BLOCK = 128
TILE = 8
CHUNK = 512
PARTS = [1024, 1024, 1024, 1024, 1024, 512, 512]
BLOCKS = [
    (0, 0), (0, 1), (0, 2), (0, 3), (1, 1),
    (1, 2), (1, 3), (2, 2), (2, 3), (3, 3),
]
HALF = 5 * BLOCK // TILE
STREAMS = [("xy", "z", 2, 0), ("yz", "x", 2, 32), ("zx", "y", 1, 64)]
VMEM_BYTES = 56 * 2**20
SHIFTS = sorted(
    [(i, j) for i in range(SIDE) for j in range(SIDE) if i or j],
    key=lambda shift: -sum(min(k, SIDE - k) for k in shift),
)
GOOD = 8e-3
ROUNDS = 4

f32, bf16 = jnp.float32, jnp.bfloat16


def dot(left, right):
    return jnp.dot(left, right, preferred_element_type=f32)


def cross(left, right):
    return lax.dot_general(left, right, (((0,), (0,)), ((), ())), preferred_element_type=f32)


def split(value):
    high = value.astype(bf16)
    return high, (value - high.astype(f32)).astype(bf16)


def dot_three(left, right):
    left_high, left_low = split(left)
    right_high, right_low = split(right)
    return dot(left_high, right_high) + (dot(left_high, right_low) + dot(left_low, right_high))


def gram_kernel(
    slab, out, held, partial, packed, core_in, rs_a, rs_b, rs_c, ln_a, ln_b, ln_c, mine_a, mine_b,
    mine_c, full, load_sem, core_sem, back_sem, rs_send, rs_recv, ln_send, ln_recv, ag_send, ag_recv,
):
    rows = slab.shape[0]
    index = lax.axis_index("rows")
    core = lax.rem(index, 2)
    here = {
        "x": lax.axis_index("group"),
        "y": lax.rem(lax.div(index, 2), SIDE),
        "z": lax.div(index, 2 * SIDE),
    }

    def device(shift):
        at = {name: lax.rem(here[name] + shift.get(name, 0), SIDE) for name in here}
        return ((at["z"] * SIDE + at["y"]) * 2 + core, at["x"])

    sibling = (index + 1 - 2 * core, here["x"])

    def load(i):
        part = pl.ds(i * CHUNK, CHUNK)
        return pltpu.make_async_copy(slab.at[part], held.at[part], load_sem.at[i])

    for i in range(rows // CHUNK):
        load(i).start()

    barrier = pltpu.get_barrier_semaphore()
    shifts = []
    for plane, _, _, _ in STREAMS:
        for i, j in SHIFTS:
            shift = {plane[0]: i, plane[1]: j}
            shift = tuple((name, shift[name]) for name in "xyz" if shift.get(name, 0))
            if shift not in shifts:
                shifts.append(shift)
    for shift in shifts:
        pl.semaphore_signal(barrier, inc=1, device_id=device(dict(shift)), device_id_type=MESH)
    pl.semaphore_signal(barrier, inc=1, device_id=sibling, device_id_type=MESH)

    for i in range(rows // CHUNK):
        load(i).wait()
        block = held[pl.ds(i * CHUNK, CHUNK), :]
        high = block.astype(bf16)
        low = ((block - high.astype(f32)) * 2.0).astype(bf16)
        term = cross(jnp.concatenate([high, high], 0), jnp.concatenate([high, low], 0))
        partial[...] = term if i == 0 else partial[...] + term

    for n, (i, j) in enumerate(BLOCKS):
        a = partial[i * BLOCK : (i + 1) * BLOCK, j * BLOCK : (j + 1) * BLOCK]
        b = partial[j * BLOCK : (j + 1) * BLOCK, i * BLOCK : (i + 1) * BLOCK]
        packed[n // 5, pl.ds((n % 5) * PLANE, PLANE)] = (a + b.T).reshape(PLANE, TILE, BLOCK)

    pl.semaphore_wait(barrier, len(shifts) + 1)

    give = pltpu.make_async_remote_copy(
        src_ref=packed.at[1 - core], dst_ref=core_in, send_sem=core_sem.at[0],
        recv_sem=core_sem.at[1], device_id=sibling, device_id_type=MESH,
    )
    give.start()
    give.wait()
    packed[core] = packed[core] + core_in[...]

    rs, ln, mine = (rs_a, rs_b, rs_c), (ln_a, ln_b, ln_c), (mine_a, mine_b, mine_c)
    spots = [here[plane[0]] * SIDE + here[plane[1]] for plane, _, _, _ in STREAMS]

    for k, (i, j) in enumerate(SHIFTS):
        for s, (plane, _, units, first) in enumerate(STREAMS):
            spot = lax.rem(here[plane[0]] + i, SIDE) * SIDE + lax.rem(here[plane[1]] + j, SIDE)
            pltpu.make_async_remote_copy(
                src_ref=packed.at[core, pl.ds(first + units * spot, units)], dst_ref=rs[s].at[k],
                send_sem=rs_send.at[s], recv_sem=rs_recv.at[s],
                device_id=device({plane[0]: i, plane[1]: j}), device_id_type=MESH,
            ).start()
    for s, (plane, line, units, first) in enumerate(STREAMS):
        pltpu.make_async_copy(rs[s], rs[s], rs_recv.at[s]).wait()
        mine[s][...] = packed[core, pl.ds(first + units * spots[s], units)] + jnp.sum(rs[s][...], axis=0)
        for k in (1, 0, 2):
            pltpu.make_async_remote_copy(
                src_ref=mine[s], dst_ref=ln[s].at[k], send_sem=ln_send.at[s],
                recv_sem=ln_recv.at[s], device_id=device({line: k + 1}), device_id_type=MESH,
            ).start()
    for s, (plane, line, units, first) in enumerate(STREAMS):
        pltpu.make_async_copy(ln[s], ln[s], ln_recv.at[s]).wait()
        place = full.at[core, pl.ds(first + units * spots[s], units)]
        place[...] = mine[s][...] + jnp.sum(ln[s][...], axis=0)
        for i, j in SHIFTS:
            pltpu.make_async_remote_copy(
                src_ref=place, dst_ref=place, send_sem=ag_send.at[s], recv_sem=ag_recv.at[s],
                device_id=device({plane[0]: i, plane[1]: j}), device_id_type=MESH,
            ).start()
    backs = []
    for s, (plane, line, units, first) in enumerate(STREAMS):
        got = full.at[core, pl.ds(first, (PLANE - 1) * units)]
        pltpu.make_async_copy(got, got, ag_recv.at[s]).wait()
        stream = full.at[core, pl.ds(first, PLANE * units)]
        back = pltpu.make_async_remote_copy(
            src_ref=stream, dst_ref=stream, send_sem=back_sem.at[0, s], recv_sem=back_sem.at[1, s],
            device_id=sibling, device_id_type=MESH,
        )
        back.start()
        backs.append(back)
    for s, (plane, line, units, first) in enumerate(STREAMS):
        sent = full.at[core, pl.ds(first, (PLANE - 1) * units)]
        pltpu.make_async_copy(rs[s], rs[s], rs_send.at[s]).wait()
        pltpu.make_async_copy(ln[s], ln[s], ln_send.at[s]).wait()
        pltpu.make_async_copy(sent, sent, ag_send.at[s]).wait()
    for back in backs:
        back.wait()
    out[...] = full[...]


def reduced_gram(slab):
    rows, width = slab.shape
    unit = lambda *lead: pltpu.VMEM((*lead, TILE, BLOCK), f32)
    dma = pltpu.SemaphoreType.DMA
    return pl.pallas_call(
        gram_kernel,
        out_shape=jax.ShapeDtypeStruct((2, HALF, TILE, BLOCK), f32),
        in_specs=[pl.BlockSpec(memory_space=pl.ANY)],
        out_specs=pl.BlockSpec(memory_space=pltpu.VMEM),
        scratch_shapes=[
            pltpu.VMEM((rows, width), f32),
            pltpu.VMEM((width, width), f32),
            unit(2, HALF),
            unit(HALF),
            *[unit(PLANE - 1, units) for _, _, units, _ in STREAMS],
            *[unit(SIDE - 1, units) for _, _, units, _ in STREAMS],
            *[unit(units) for _, _, units, _ in STREAMS],
            unit(2, HALF),
            dma((rows // CHUNK,)),
            dma((2,)),
            dma((2, 3)),
            *[dma((3,)) for _ in range(6)],
        ],
        compiler_params=pltpu.CompilerParams(
            collective_id=0, has_side_effects=True, vmem_limit_bytes=VMEM_BYTES
        ),
    )(slab)


def apply_kernel(
    scale, gram, slab, out, held, ready, shifted, work, mixing, load_sem, store_sem
):
    rows, width = slab.shape

    load = pltpu.make_async_copy(slab, held, load_sem)
    load.start()

    row_ids = lax.broadcasted_iota(jnp.int32, (width, width), 0)
    col_ids = lax.broadcasted_iota(jnp.int32, (width, width), 1)
    identity = (row_ids == col_ids).astype(f32)
    for n, (i, j) in enumerate(BLOCKS):
        a = gram[n // 5, pl.ds((n % 5) * PLANE, PLANE)].reshape(BLOCK, BLOCK)
        shifted[i * BLOCK : (i + 1) * BLOCK, j * BLOCK : (j + 1) * BLOCK] = a
        if i != j:
            shifted[j * BLOCK : (j + 1) * BLOCK, i * BLOCK : (i + 1) * BLOCK] = a.T
    matrix = shifted[...] * scale + identity

    diagonal = matrix * identity
    diagonal_row = jnp.sum(diagonal, axis=0, keepdims=True)
    diagonal_col = jnp.sum(diagonal, axis=1, keepdims=True)
    by_row, by_col = lax.rsqrt(diagonal_row), lax.rsqrt(diagonal_col)
    matrix = matrix * by_row * by_col
    shifted[...] = matrix
    low = 1.0 / jnp.max(diagonal_row, axis=1, keepdims=True)
    sums = jnp.sum(jnp.abs(matrix), axis=0, keepdims=True)
    high = jnp.maximum(jnp.max(sums, axis=1, keepdims=True) * 1.01, 4.0 * low)

    gap = 1.0 / (high - low)
    t = (high + low) * gap
    cheb = t * identity - (2.0 * gap) * matrix
    cheb_16 = cheb.astype(bf16)
    t_next = 2.0 * t * t - 1.0
    inverse = (4.0 * t / (t_next * (high + low))) * (t * identity + cheb)
    cheb = 2.0 * dot(cheb_16, cheb_16) - identity
    t = t_next
    for n in range(ROUNDS):
        t_next = 2.0 * t * t - 1.0
        cheb_16, inverse_16 = cheb.astype(bf16), inverse.astype(bf16)
        if n < ROUNDS - 1:
            product = dot(jnp.concatenate([inverse_16, cheb_16], 0), cheb_16)
            cheb = 2.0 * product[width:] - identity
            product = product[:width]
        else:
            product = dot(inverse_16, cheb_16)
        inverse = (2.0 * t / t_next) * (t * inverse + product)
        t = t_next

    matrix_high, matrix_low = split(shifted[...])
    inverse_16 = inverse.astype(bf16)
    residual = identity - (dot(matrix_high, inverse_16) + dot(matrix_low, inverse_16))
    inverse = inverse_16.astype(f32) + dot(inverse_16, residual.astype(bf16))

    def refine(inverse):
        residual = identity - dot_three(shifted[...], inverse)
        work[...] = inverse + dot(inverse.astype(bf16), residual.astype(bf16))
        return jnp.sum(residual * residual)

    def unfinished(carry):
        size, n = carry
        return jnp.logical_and(size > GOOD * GOOD, n < 8)

    size = refine(inverse)
    size, _ = lax.while_loop(unfinished, lambda carry: (refine(work[...]), carry[1] + 1), (size, 0))

    @pl.when(jnp.logical_not(size <= GOOD * GOOD))
    def _():
        work[...] = shifted[...]

        def eliminate(k, carry):
            value = work[...]
            row = work[pl.ds(k, 1), :]
            at_col = col_ids == k
            col = jnp.sum(jnp.where(at_col, value, 0.0), axis=1, keepdims=True)
            pivot = 1.0 / jnp.sum(jnp.where(at_col[:1], row, 0.0), axis=1, keepdims=True)
            row = jnp.where(at_col[:1], pivot, row * pivot)
            value = jnp.where(at_col, 0.0, value) - col * row
            work[...] = jnp.where(row_ids == k, row, value)
            return carry

        lax.fori_loop(0, width, eliminate, 0)

    constant, factor = weight_beta / weight_gamma, weight_alpha - weight_beta / weight_gamma
    inverse = work[...] * by_row * by_col
    mixing[...] = constant * identity + factor * inverse

    load.wait()

    def store(n):
        part = pl.ds(sum(PARTS[:n]), PARTS[n])
        return pltpu.make_async_copy(ready.at[part], out.at[part], store_sem.at[n])

    mixing_high, mixing_low = split(mixing[...])
    for n in range(len(PARTS)):
        part = pl.ds(sum(PARTS[:n]), PARTS[n])
        high_part, low_part = split(held[part, :])
        ready[part, :] = dot(high_part, mixing_high) + (
            dot(high_part, mixing_low) + dot(low_part, mixing_high)
        )
        store(n).start()
    for n in range(len(PARTS)):
        store(n).wait()


def applied(scale, gram, slab):
    rows, width = slab.shape
    dma = pltpu.SemaphoreType.DMA
    return pl.pallas_call(
        functools.partial(apply_kernel, scale),
        out_shape=jax.ShapeDtypeStruct((rows, width), f32),
        in_specs=[pl.BlockSpec(memory_space=pltpu.VMEM), pl.BlockSpec(memory_space=pl.ANY)],
        out_specs=pl.BlockSpec(memory_space=pl.ANY),
        scratch_shapes=[
            pltpu.VMEM((rows, width), f32),
            pltpu.VMEM((rows, width), f32),
            pltpu.VMEM((width, width), f32),
            pltpu.VMEM((width, width), f32),
            pltpu.VMEM((width, width), f32),
            dma,
            dma((len(PARTS),)),
        ],
        compiler_params=pltpu.CompilerParams(vmem_limit_bytes=VMEM_BYTES),
    )(gram, slab)


def local(slab):
    devices_all = lax.axis_size("rows") * lax.axis_size("group")
    scale = 0.5 * weight_gamma / (slab.shape[0] * devices_all)
    return applied(scale, reduced_gram(slab), slab)


def solution(mesh):
    placed = (P(("rows", "group"), None),)
    return jax.shard_map(
        local, mesh=mesh, in_specs=placed, out_specs=P(("rows", "group"), None), check_vma=False
    )
```

```python
import functools
import math

import jax
import jax.numpy as jnp
from jax import lax
from jax.experimental import pallas as pl
from jax.experimental.pallas import tpu as pltpu
from jax.sharding import PartitionSpec as P

lower_bound = 0.1
spread_d = (4.0 * (1.0 - lower_bound**2) / lower_bound**4) ** (1.0 / 3.0)
weight_alpha = math.sqrt(1.0 + spread_d) + 0.5 * math.sqrt(
    8.0
    - 4.0 * spread_d
    + 8.0 * (2.0 - lower_bound**2) / (lower_bound**2 * math.sqrt(1.0 + spread_d))
)
weight_beta = (weight_alpha - 1.0) ** 2 / 4.0
weight_gamma = weight_alpha + weight_beta - 1.0

MESH = pl.DeviceIdType.MESH
SIDE = 4
PLANE = SIDE * SIDE
BLOCK = 128
TILE = 8
LOADS = [256, 512, 768, 1024, 1024, 1024, 1536]
STORES = [1024, 1024, 1024, 1024, 1024, 512, 512]
BLOCKS = [
    (0, 0), (0, 1), (0, 2), (0, 3), (1, 1),
    (1, 2), (1, 3), (2, 2), (2, 3), (3, 3),
]
HALF = 5 * BLOCK // TILE
STREAMS = [("xy", "z", 2, 0), ("yz", "x", 2, 32), ("zx", "y", 1, 64)]
VMEM_BYTES = 50 * 2**20
SHIFTS = sorted(
    [(i, j) for i in range(SIDE) for j in range(SIDE) if i or j],
    key=lambda shift: -sum(min(k, SIDE - k) for k in shift),
)
GOOD = 8e-3
ROUNDS = 4

f32, bf16 = jnp.float32, jnp.bfloat16


def dot(left, right):
    return jnp.dot(left, right, preferred_element_type=f32)


def cross(left, right):
    return lax.dot_general(left, right, (((0,), (0,)), ((), ())), preferred_element_type=f32)


def split(value):
    high = value.astype(bf16)
    return high, (value - high.astype(f32)).astype(bf16)


def dot_three(left, right):
    left_high, left_low = split(left)
    right_high, right_low = split(right)
    return dot(left_high, right_high) + (dot(left_high, right_low) + dot(left_low, right_high))


def gram_kernel(
    slab, out, held, partial, packed, core_in, rs_a, rs_b, rs_c, ln_a, ln_b, ln_c, mine_a, mine_b,
    mine_c, full, load_sem, core_sem, back_sem, rs_send, rs_recv, ln_send, ln_recv, ag_send, ag_recv,
):
    index = lax.axis_index("rows")
    core = lax.rem(index, 2)
    here = {
        "x": lax.axis_index("group"),
        "y": lax.rem(lax.div(index, 2), SIDE),
        "z": lax.div(index, 2 * SIDE),
    }

    def device(shift):
        at = {name: lax.rem(here[name] + shift.get(name, 0), SIDE) for name in here}
        return ((at["z"] * SIDE + at["y"]) * 2 + core, at["x"])

    sibling = (index + 1 - 2 * core, here["x"])

    def load(i):
        part = pl.ds(sum(LOADS[:i]), LOADS[i])
        return pltpu.make_async_copy(slab.at[part], held.at[part], load_sem.at[i])

    for i in range(len(LOADS)):
        load(i).start()

    barrier = pltpu.get_barrier_semaphore()
    shifts = []
    for plane, _, _, _ in STREAMS:
        for i, j in SHIFTS:
            shift = {plane[0]: i, plane[1]: j}
            shift = tuple((name, shift[name]) for name in "xyz" if shift.get(name, 0))
            if shift not in shifts:
                shifts.append(shift)
    for shift in shifts:
        pl.semaphore_signal(barrier, inc=1, device_id=device(dict(shift)), device_id_type=MESH)
    pl.semaphore_signal(barrier, inc=1, device_id=sibling, device_id_type=MESH)

    for i in range(len(LOADS)):
        load(i).wait()
        block = held[pl.ds(sum(LOADS[:i]), LOADS[i]), :]
        high = block.astype(bf16)
        low = ((block - high.astype(f32)) * 2.0).astype(bf16)
        term = cross(jnp.concatenate([high, high], 0), jnp.concatenate([high, low], 0))
        partial[...] = term if i == 0 else partial[...] + term

    for n, (i, j) in enumerate(BLOCKS):
        a = partial[i * BLOCK : (i + 1) * BLOCK, j * BLOCK : (j + 1) * BLOCK]
        b = partial[j * BLOCK : (j + 1) * BLOCK, i * BLOCK : (i + 1) * BLOCK]
        packed[n // 5, pl.ds((n % 5) * PLANE, PLANE)] = (a + b.T).reshape(PLANE, TILE, BLOCK)

    pl.semaphore_wait(barrier, len(shifts) + 1)

    give = pltpu.make_async_remote_copy(
        src_ref=packed.at[1 - core], dst_ref=core_in, send_sem=core_sem.at[0],
        recv_sem=core_sem.at[1], device_id=sibling, device_id_type=MESH,
    )
    give.start()
    give.wait()
    packed[core] = packed[core] + core_in[...]

    rs, ln, mine = (rs_a, rs_b, rs_c), (ln_a, ln_b, ln_c), (mine_a, mine_b, mine_c)
    spots = [here[plane[0]] * SIDE + here[plane[1]] for plane, _, _, _ in STREAMS]

    for k, (i, j) in enumerate(SHIFTS):
        for s, (plane, _, units, first) in enumerate(STREAMS):
            spot = lax.rem(here[plane[0]] + i, SIDE) * SIDE + lax.rem(here[plane[1]] + j, SIDE)
            pltpu.make_async_remote_copy(
                src_ref=packed.at[core, pl.ds(first + units * spot, units)], dst_ref=rs[s].at[k],
                send_sem=rs_send.at[s], recv_sem=rs_recv.at[s],
                device_id=device({plane[0]: i, plane[1]: j}), device_id_type=MESH,
            ).start()
    for s, (plane, line, units, first) in enumerate(STREAMS):
        pltpu.make_async_copy(rs[s], rs[s], rs_recv.at[s]).wait()
        mine[s][...] = packed[core, pl.ds(first + units * spots[s], units)] + jnp.sum(rs[s][...], axis=0)
        for k in (1, 0, 2):
            pltpu.make_async_remote_copy(
                src_ref=mine[s], dst_ref=ln[s].at[k], send_sem=ln_send.at[s],
                recv_sem=ln_recv.at[s], device_id=device({line: k + 1}), device_id_type=MESH,
            ).start()
    for s, (plane, line, units, first) in enumerate(STREAMS):
        pltpu.make_async_copy(ln[s], ln[s], ln_recv.at[s]).wait()
        place = full.at[core, pl.ds(first + units * spots[s], units)]
        place[...] = mine[s][...] + jnp.sum(ln[s][...], axis=0)
        for i, j in SHIFTS:
            pltpu.make_async_remote_copy(
                src_ref=place, dst_ref=place, send_sem=ag_send.at[s], recv_sem=ag_recv.at[s],
                device_id=device({plane[0]: i, plane[1]: j}), device_id_type=MESH,
            ).start()
    backs = []
    for s, (plane, line, units, first) in enumerate(STREAMS):
        got = full.at[core, pl.ds(first, (PLANE - 1) * units)]
        pltpu.make_async_copy(got, got, ag_recv.at[s]).wait()
        stream = full.at[core, pl.ds(first, PLANE * units)]
        back = pltpu.make_async_remote_copy(
            src_ref=stream, dst_ref=stream, send_sem=back_sem.at[0, s], recv_sem=back_sem.at[1, s],
            device_id=sibling, device_id_type=MESH,
        )
        back.start()
        backs.append(back)
    for s, (plane, line, units, first) in enumerate(STREAMS):
        sent = full.at[core, pl.ds(first, (PLANE - 1) * units)]
        pltpu.make_async_copy(rs[s], rs[s], rs_send.at[s]).wait()
        pltpu.make_async_copy(ln[s], ln[s], ln_send.at[s]).wait()
        pltpu.make_async_copy(sent, sent, ag_send.at[s]).wait()
    for back in backs:
        back.wait()
    out[...] = full[...]


def reduced_gram(slab):
    rows, width = slab.shape
    unit = lambda *lead: pltpu.VMEM((*lead, TILE, BLOCK), f32)
    dma = pltpu.SemaphoreType.DMA
    return pl.pallas_call(
        gram_kernel,
        out_shape=jax.ShapeDtypeStruct((2, HALF, TILE, BLOCK), f32),
        in_specs=[pl.BlockSpec(memory_space=pl.ANY)],
        out_specs=pl.BlockSpec(memory_space=pltpu.VMEM),
        scratch_shapes=[
            pltpu.VMEM((rows, width), f32),
            pltpu.VMEM((width, width), f32),
            unit(2, HALF),
            unit(HALF),
            *[unit(PLANE - 1, units) for _, _, units, _ in STREAMS],
            *[unit(SIDE - 1, units) for _, _, units, _ in STREAMS],
            *[unit(units) for _, _, units, _ in STREAMS],
            unit(2, HALF),
            dma((len(LOADS),)),
            dma((2,)),
            dma((2, 3)),
            *[dma((3,)) for _ in range(6)],
        ],
        compiler_params=pltpu.CompilerParams(
            collective_id=0, has_side_effects=True, vmem_limit_bytes=VMEM_BYTES
        ),
    )(slab)


def apply_kernel(
    scale, gram, slab, out, held, ready, shifted, work, mixing, load_sem, store_sem
):
    rows, width = slab.shape

    load = pltpu.make_async_copy(slab, held, load_sem)
    load.start()

    row_ids = lax.broadcasted_iota(jnp.int32, (width, width), 0)
    col_ids = lax.broadcasted_iota(jnp.int32, (width, width), 1)
    identity = (row_ids == col_ids).astype(f32)
    for n, (i, j) in enumerate(BLOCKS):
        a = gram[n // 5, pl.ds((n % 5) * PLANE, PLANE)].reshape(BLOCK, BLOCK)
        shifted[i * BLOCK : (i + 1) * BLOCK, j * BLOCK : (j + 1) * BLOCK] = a
        if i != j:
            shifted[j * BLOCK : (j + 1) * BLOCK, i * BLOCK : (i + 1) * BLOCK] = a.T
    matrix = shifted[...] * scale + identity

    diagonal = matrix * identity
    diagonal_row = jnp.sum(diagonal, axis=0, keepdims=True)
    diagonal_col = jnp.sum(diagonal, axis=1, keepdims=True)
    by_row, by_col = lax.rsqrt(diagonal_row), lax.rsqrt(diagonal_col)
    matrix = matrix * by_row * by_col
    shifted[...] = matrix
    low = 1.0 / jnp.max(diagonal_row, axis=1, keepdims=True)
    sums = jnp.sum(jnp.abs(matrix), axis=0, keepdims=True)
    high = jnp.maximum(jnp.max(sums, axis=1, keepdims=True) * 1.01, 4.0 * low)

    gap = 1.0 / (high - low)
    t = (high + low) * gap
    cheb = t * identity - (2.0 * gap) * matrix
    cheb_16 = cheb.astype(bf16)
    t_next = 2.0 * t * t - 1.0
    inverse = (4.0 * t / (t_next * (high + low))) * (t * identity + cheb)
    cheb = 2.0 * dot(cheb_16, cheb_16) - identity
    t = t_next
    for n in range(ROUNDS):
        t_next = 2.0 * t * t - 1.0
        cheb_16, inverse_16 = cheb.astype(bf16), inverse.astype(bf16)
        if n < ROUNDS - 1:
            product = dot(jnp.concatenate([inverse_16, cheb_16], 0), cheb_16)
            cheb = 2.0 * product[width:] - identity
            product = product[:width]
        else:
            product = dot(inverse_16, cheb_16)
        inverse = (2.0 * t / t_next) * (t * inverse + product)
        t = t_next

    matrix_high, matrix_low = split(shifted[...])
    inverse_16 = inverse.astype(bf16)
    residual = identity - (dot(matrix_high, inverse_16) + dot(matrix_low, inverse_16))
    residual_16 = residual.astype(bf16)
    residual = residual + dot(residual_16, residual_16)
    inverse = inverse_16.astype(f32) + dot(inverse_16, residual.astype(bf16))

    def refine(inverse):
        residual = identity - dot_three(shifted[...], inverse)
        work[...] = inverse + dot(inverse.astype(bf16), residual.astype(bf16))
        return jnp.sum(residual * residual)

    def unfinished(carry):
        size, n = carry
        return jnp.logical_and(size > GOOD * GOOD, n < 8)

    size = refine(inverse)
    size, _ = lax.while_loop(unfinished, lambda carry: (refine(work[...]), carry[1] + 1), (size, 0))

    @pl.when(jnp.logical_not(size <= GOOD * GOOD))
    def _():
        work[...] = shifted[...]

        def eliminate(k, carry):
            value = work[...]
            row = work[pl.ds(k, 1), :]
            at_col = col_ids == k
            col = jnp.sum(jnp.where(at_col, value, 0.0), axis=1, keepdims=True)
            pivot = 1.0 / jnp.sum(jnp.where(at_col[:1], row, 0.0), axis=1, keepdims=True)
            row = jnp.where(at_col[:1], pivot, row * pivot)
            value = jnp.where(at_col, 0.0, value) - col * row
            work[...] = jnp.where(row_ids == k, row, value)
            return carry

        lax.fori_loop(0, width, eliminate, 0)

    constant, factor = weight_beta / weight_gamma, weight_alpha - weight_beta / weight_gamma
    inverse = work[...] * by_row * by_col
    mixing[...] = constant * identity + factor * inverse

    load.wait()

    def store(n):
        part = pl.ds(sum(STORES[:n]), STORES[n])
        return pltpu.make_async_copy(ready.at[part], out.at[part], store_sem.at[n])

    mixing_high, mixing_low = split(mixing[...])
    for n in range(len(STORES)):
        part = pl.ds(sum(STORES[:n]), STORES[n])
        high_part, low_part = split(held[part, :])
        ready[part, :] = dot(high_part, mixing_high) + (
            dot(high_part, mixing_low) + dot(low_part, mixing_high)
        )
        store(n).start()
    for n in range(len(STORES)):
        store(n).wait()


def applied(scale, gram, slab):
    rows, width = slab.shape
    dma = pltpu.SemaphoreType.DMA
    return pl.pallas_call(
        functools.partial(apply_kernel, scale),
        out_shape=jax.ShapeDtypeStruct((rows, width), f32),
        in_specs=[pl.BlockSpec(memory_space=pltpu.VMEM), pl.BlockSpec(memory_space=pl.ANY)],
        out_specs=pl.BlockSpec(memory_space=pl.ANY),
        scratch_shapes=[
            pltpu.VMEM((rows, width), f32),
            pltpu.VMEM((rows, width), f32),
            pltpu.VMEM((width, width), f32),
            pltpu.VMEM((width, width), f32),
            pltpu.VMEM((width, width), f32),
            dma,
            dma((len(STORES),)),
        ],
        compiler_params=pltpu.CompilerParams(vmem_limit_bytes=VMEM_BYTES),
    )(gram, slab)


def local(slab):
    devices_all = lax.axis_size("rows") * lax.axis_size("group")
    scale = 0.5 * weight_gamma / (slab.shape[0] * devices_all)
    return applied(scale, reduced_gram(slab), slab)


def solution(mesh):
    placed = (P(("rows", "group"), None),)
    return jax.shard_map(
        local, mesh=mesh, in_specs=placed, out_specs=P(("rows", "group"), None), check_vma=False
    )
```

```python
import functools
import math

import jax
import jax.numpy as jnp
from jax import lax
from jax.experimental import pallas as pl
from jax.experimental.pallas import tpu as pltpu
from jax.sharding import PartitionSpec as P

lower_bound = 0.1
spread_d = (4.0 * (1.0 - lower_bound**2) / lower_bound**4) ** (1.0 / 3.0)
weight_alpha = math.sqrt(1.0 + spread_d) + 0.5 * math.sqrt(
    8.0
    - 4.0 * spread_d
    + 8.0 * (2.0 - lower_bound**2) / (lower_bound**2 * math.sqrt(1.0 + spread_d))
)
weight_beta = (weight_alpha - 1.0) ** 2 / 4.0
weight_gamma = weight_alpha + weight_beta - 1.0

MESH = pl.DeviceIdType.MESH
SIDE = 4
PLANE = SIDE * SIDE
BLOCK = 128
TILE = 8
LOADS = [256, 512, 768, 1024, 1024, 1024, 1536]
STORES = [1024, 1024, 1024, 1024, 1024, 512, 512]
BLOCKS = [
    (0, 0), (0, 1), (0, 2), (0, 3), (1, 1),
    (1, 2), (1, 3), (2, 2), (2, 3), (3, 3),
]
HALF = 5 * BLOCK // TILE
STREAMS = [("xy", "z", 2, 0), ("yz", "x", 2, 32), ("zx", "y", 1, 64)]
VMEM_BYTES = 50 * 2**20
SHIFTS = sorted(
    [(i, j) for i in range(SIDE) for j in range(SIDE) if i or j],
    key=lambda shift: -sum(min(k, SIDE - k) for k in shift),
)
GOOD = 8e-3
LOW_SCALE = 512.0
MOST_SPREAD = 1.5
LEAST_COLUMN = 1 / 32
ROUNDS = 4

f32, bf16, f8 = jnp.float32, jnp.bfloat16, jnp.float8_e4m3fn


def dot(left, right):
    return jnp.dot(left, right, preferred_element_type=f32)


def cross(left, right):
    return lax.dot_general(left, right, (((0,), (0,)), ((), ())), preferred_element_type=f32)


def split(value):
    high = value.astype(bf16)
    return high, (value - high.astype(f32)).astype(bf16)


def dot_three(left, right):
    left_high, left_low = split(left)
    right_high, right_low = split(right)
    return dot(left_high, right_high) + (dot(left_high, right_low) + dot(left_low, right_high))


def gram_kernel(
    slab, out, held, partial, packed, core_in, rs_a, rs_b, rs_c, ln_a, ln_b, ln_c, mine_a, mine_b,
    mine_c, full, load_sem, core_sem, back_sem, rs_send, rs_recv, ln_send, ln_recv, ag_send, ag_recv,
):
    index = lax.axis_index("rows")
    core = lax.rem(index, 2)
    here = {
        "x": lax.axis_index("group"),
        "y": lax.rem(lax.div(index, 2), SIDE),
        "z": lax.div(index, 2 * SIDE),
    }

    def device(shift):
        at = {name: lax.rem(here[name] + shift.get(name, 0), SIDE) for name in here}
        return ((at["z"] * SIDE + at["y"]) * 2 + core, at["x"])

    sibling = (index + 1 - 2 * core, here["x"])

    def load(i):
        part = pl.ds(sum(LOADS[:i]), LOADS[i])
        return pltpu.make_async_copy(slab.at[part], held.at[part], load_sem.at[i])

    for i in range(len(LOADS)):
        load(i).start()

    barrier = pltpu.get_barrier_semaphore()
    shifts = []
    for plane, _, _, _ in STREAMS:
        for i, j in SHIFTS:
            shift = {plane[0]: i, plane[1]: j}
            shift = tuple((name, shift[name]) for name in "xyz" if shift.get(name, 0))
            if shift not in shifts:
                shifts.append(shift)
    for shift in shifts:
        pl.semaphore_signal(barrier, inc=1, device_id=device(dict(shift)), device_id_type=MESH)
    pl.semaphore_signal(barrier, inc=1, device_id=sibling, device_id_type=MESH)

    for i in range(len(LOADS)):
        load(i).wait()
        block = held[pl.ds(sum(LOADS[:i]), LOADS[i]), :]
        high = block.astype(bf16)
        low = ((block - high.astype(f32)) * 2.0).astype(bf16)
        term = cross(jnp.concatenate([high, high], 0), jnp.concatenate([high, low], 0))
        partial[...] = term if i == 0 else partial[...] + term

    for n, (i, j) in enumerate(BLOCKS):
        a = partial[i * BLOCK : (i + 1) * BLOCK, j * BLOCK : (j + 1) * BLOCK]
        b = partial[j * BLOCK : (j + 1) * BLOCK, i * BLOCK : (i + 1) * BLOCK]
        packed[n // 5, pl.ds((n % 5) * PLANE, PLANE)] = (a + b.T).reshape(PLANE, TILE, BLOCK)

    pl.semaphore_wait(barrier, len(shifts) + 1)

    give = pltpu.make_async_remote_copy(
        src_ref=packed.at[1 - core], dst_ref=core_in, send_sem=core_sem.at[0],
        recv_sem=core_sem.at[1], device_id=sibling, device_id_type=MESH,
    )
    give.start()
    give.wait()
    packed[core] = packed[core] + core_in[...]

    rs, ln, mine = (rs_a, rs_b, rs_c), (ln_a, ln_b, ln_c), (mine_a, mine_b, mine_c)
    spots = [here[plane[0]] * SIDE + here[plane[1]] for plane, _, _, _ in STREAMS]

    for k, (i, j) in enumerate(SHIFTS):
        for s, (plane, _, units, first) in enumerate(STREAMS):
            spot = lax.rem(here[plane[0]] + i, SIDE) * SIDE + lax.rem(here[plane[1]] + j, SIDE)
            pltpu.make_async_remote_copy(
                src_ref=packed.at[core, pl.ds(first + units * spot, units)], dst_ref=rs[s].at[k],
                send_sem=rs_send.at[s], recv_sem=rs_recv.at[s],
                device_id=device({plane[0]: i, plane[1]: j}), device_id_type=MESH,
            ).start()
    for s, (plane, line, units, first) in enumerate(STREAMS):
        pltpu.make_async_copy(rs[s], rs[s], rs_recv.at[s]).wait()
        mine[s][...] = packed[core, pl.ds(first + units * spots[s], units)] + jnp.sum(rs[s][...], axis=0)
        for k in (1, 0, 2):
            pltpu.make_async_remote_copy(
                src_ref=mine[s], dst_ref=ln[s].at[k], send_sem=ln_send.at[s],
                recv_sem=ln_recv.at[s], device_id=device({line: k + 1}), device_id_type=MESH,
            ).start()
    for s, (plane, line, units, first) in enumerate(STREAMS):
        pltpu.make_async_copy(ln[s], ln[s], ln_recv.at[s]).wait()
        place = full.at[core, pl.ds(first + units * spots[s], units)]
        place[...] = mine[s][...] + jnp.sum(ln[s][...], axis=0)
        for i, j in SHIFTS:
            pltpu.make_async_remote_copy(
                src_ref=place, dst_ref=place, send_sem=ag_send.at[s], recv_sem=ag_recv.at[s],
                device_id=device({plane[0]: i, plane[1]: j}), device_id_type=MESH,
            ).start()
    backs = []
    for s, (plane, line, units, first) in enumerate(STREAMS):
        got = full.at[core, pl.ds(first, (PLANE - 1) * units)]
        pltpu.make_async_copy(got, got, ag_recv.at[s]).wait()
        stream = full.at[core, pl.ds(first, PLANE * units)]
        back = pltpu.make_async_remote_copy(
            src_ref=stream, dst_ref=stream, send_sem=back_sem.at[0, s], recv_sem=back_sem.at[1, s],
            device_id=sibling, device_id_type=MESH,
        )
        back.start()
        backs.append(back)
    for s, (plane, line, units, first) in enumerate(STREAMS):
        sent = full.at[core, pl.ds(first, (PLANE - 1) * units)]
        pltpu.make_async_copy(rs[s], rs[s], rs_send.at[s]).wait()
        pltpu.make_async_copy(ln[s], ln[s], ln_send.at[s]).wait()
        pltpu.make_async_copy(sent, sent, ag_send.at[s]).wait()
    for back in backs:
        back.wait()
    out[...] = full[...]


def reduced_gram(slab):
    rows, width = slab.shape
    unit = lambda *lead: pltpu.VMEM((*lead, TILE, BLOCK), f32)
    dma = pltpu.SemaphoreType.DMA
    return pl.pallas_call(
        gram_kernel,
        out_shape=jax.ShapeDtypeStruct((2, HALF, TILE, BLOCK), f32),
        in_specs=[pl.BlockSpec(memory_space=pl.ANY)],
        out_specs=pl.BlockSpec(memory_space=pltpu.VMEM),
        scratch_shapes=[
            pltpu.VMEM((rows, width), f32),
            pltpu.VMEM((width, width), f32),
            unit(2, HALF),
            unit(HALF),
            *[unit(PLANE - 1, units) for _, _, units, _ in STREAMS],
            *[unit(SIDE - 1, units) for _, _, units, _ in STREAMS],
            *[unit(units) for _, _, units, _ in STREAMS],
            unit(2, HALF),
            dma((len(LOADS),)),
            dma((2,)),
            dma((2, 3)),
            *[dma((3,)) for _ in range(6)],
        ],
        compiler_params=pltpu.CompilerParams(
            collective_id=0, has_side_effects=True, vmem_limit_bytes=VMEM_BYTES
        ),
    )(slab)


def apply_kernel(
    scale, gram, slab, out, held, ready, shifted, work, mixing, load_sem, store_sem
):
    rows, width = slab.shape

    load = pltpu.make_async_copy(slab, held, load_sem)
    load.start()

    row_ids = lax.broadcasted_iota(jnp.int32, (width, width), 0)
    col_ids = lax.broadcasted_iota(jnp.int32, (width, width), 1)
    identity = (row_ids == col_ids).astype(f32)
    for n, (i, j) in enumerate(BLOCKS):
        a = gram[n // 5, pl.ds((n % 5) * PLANE, PLANE)].reshape(BLOCK, BLOCK)
        shifted[i * BLOCK : (i + 1) * BLOCK, j * BLOCK : (j + 1) * BLOCK] = a
        if i != j:
            shifted[j * BLOCK : (j + 1) * BLOCK, i * BLOCK : (i + 1) * BLOCK] = a.T
    matrix = shifted[...] * scale + identity

    diagonal = matrix * identity
    diagonal_row = jnp.sum(diagonal, axis=0, keepdims=True)
    diagonal_col = jnp.sum(diagonal, axis=1, keepdims=True)
    by_row, by_col = lax.rsqrt(diagonal_row), lax.rsqrt(diagonal_col)
    matrix = matrix * by_row * by_col
    shifted[...] = matrix
    low = 1.0 / jnp.max(diagonal_row, axis=1, keepdims=True)
    sums = jnp.sum(jnp.abs(matrix), axis=0, keepdims=True)
    high = jnp.maximum(jnp.max(sums, axis=1, keepdims=True) * 1.01, 4.0 * low)

    gap = 1.0 / (high - low)
    t = (high + low) * gap
    cheb = t * identity - (2.0 * gap) * matrix
    cheb_16 = cheb.astype(bf16)
    t_next = 2.0 * t * t - 1.0
    inverse = (4.0 * t / (t_next * (high + low))) * (t * identity + cheb)
    cheb = 2.0 * dot(cheb_16, cheb_16) - identity
    t = t_next
    for n in range(ROUNDS):
        t_next = 2.0 * t * t - 1.0
        cheb_16, inverse_16 = cheb.astype(bf16), inverse.astype(bf16)
        if n < ROUNDS - 1:
            product = dot(jnp.concatenate([inverse_16, cheb_16], 0), cheb_16)
            cheb = 2.0 * product[width:] - identity
            product = product[:width]
        else:
            product = dot(inverse_16, cheb_16)
        inverse = (2.0 * t / t_next) * (t * inverse + product)
        t = t_next

    matrix_high, matrix_low = split(shifted[...])
    inverse_16 = inverse.astype(bf16)
    residual = identity - (dot(matrix_high, inverse_16) + dot(matrix_low, inverse_16))
    residual_16 = residual.astype(bf16)
    residual = residual + dot(residual_16, residual_16)
    inverse = inverse_16.astype(f32) + dot(inverse_16, residual.astype(bf16))

    def refine(inverse):
        residual = identity - dot_three(shifted[...], inverse)
        work[...] = inverse + dot(inverse.astype(bf16), residual.astype(bf16))
        return jnp.sum(residual * residual)

    def unfinished(carry):
        size, n = carry
        return jnp.logical_and(size > GOOD * GOOD, n < 8)

    size = refine(inverse)
    size, _ = lax.while_loop(unfinished, lambda carry: (refine(work[...]), carry[1] + 1), (size, 0))

    @pl.when(jnp.logical_not(size <= GOOD * GOOD))
    def _():
        work[...] = shifted[...]

        def eliminate(k, carry):
            value = work[...]
            row = work[pl.ds(k, 1), :]
            at_col = col_ids == k
            col = jnp.sum(jnp.where(at_col, value, 0.0), axis=1, keepdims=True)
            pivot = 1.0 / jnp.sum(jnp.where(at_col[:1], row, 0.0), axis=1, keepdims=True)
            row = jnp.where(at_col[:1], pivot, row * pivot)
            value = jnp.where(at_col, 0.0, value) - col * row
            work[...] = jnp.where(row_ids == k, row, value)
            return carry

        lax.fori_loop(0, width, eliminate, 0)

    constant, factor = weight_beta / weight_gamma, weight_alpha - weight_beta / weight_gamma
    inverse = work[...] * by_row * by_col
    mixed = constant * identity + factor * inverse
    inverse_diagonal = jnp.sum(inverse * identity, axis=0, keepdims=True)
    mixing_diagonal = constant + factor * inverse_diagonal
    off_diagonal = mixed * (1.0 - identity)
    mixing[...] = mixed

    spread = jnp.sum((diagonal_col - 1.0) * off_diagonal * off_diagonal)
    trace, trace_inverse = jnp.sum(diagonal_row), jnp.sum(inverse_diagonal)
    total = (
        constant**2 * (trace - width)
        + 2.0 * constant * factor * (width - trace_inverse)
        + factor**2 * (trace_inverse - jnp.sum(inverse * inverse))
    )
    mild = jnp.logical_and(
        spread <= MOST_SPREAD * total,
        jnp.min(diagonal_row) >= 1.0 + weight_gamma * LEAST_COLUMN**2,
    )
    load.wait()

    def store(n):
        part = pl.ds(sum(STORES[:n]), STORES[n])
        return pltpu.make_async_copy(ready.at[part], out.at[part], store_sem.at[n])

    @pl.when(mild)
    def _():
        mixing_high, mixing_low = split(off_diagonal)
        mixing_8 = (mixing_low.astype(f32) * LOW_SCALE).astype(f8)
        for n in range(len(STORES)):
            part = pl.ds(sum(STORES[:n]), STORES[n])
            block = held[part, :]
            high_part, low_part = split(block)
            ready[part, :] = block * mixing_diagonal + (
                dot(high_part, mixing_high)
                + dot(low_part, mixing_high)
                + dot(high_part.astype(f8), mixing_8) * (1.0 / LOW_SCALE)
            )
            store(n).start()

    @pl.when(jnp.logical_not(mild))
    def _():
        for n in range(len(STORES)):
            part = pl.ds(sum(STORES[:n]), STORES[n])
            ready[part, :] = dot_three(held[part, :], mixing[...])
            store(n).start()

    for n in range(len(STORES)):
        store(n).wait()


def applied(scale, gram, slab):
    rows, width = slab.shape
    dma = pltpu.SemaphoreType.DMA
    return pl.pallas_call(
        functools.partial(apply_kernel, scale),
        out_shape=jax.ShapeDtypeStruct((rows, width), f32),
        in_specs=[pl.BlockSpec(memory_space=pltpu.VMEM), pl.BlockSpec(memory_space=pl.ANY)],
        out_specs=pl.BlockSpec(memory_space=pl.ANY),
        scratch_shapes=[
            pltpu.VMEM((rows, width), f32),
            pltpu.VMEM((rows, width), f32),
            pltpu.VMEM((width, width), f32),
            pltpu.VMEM((width, width), f32),
            pltpu.VMEM((width, width), f32),
            dma,
            dma((len(STORES),)),
        ],
        compiler_params=pltpu.CompilerParams(vmem_limit_bytes=VMEM_BYTES),
    )(gram, slab)


def local(slab):
    devices_all = lax.axis_size("rows") * lax.axis_size("group")
    scale = 0.5 * weight_gamma / (slab.shape[0] * devices_all)
    return applied(scale, reduced_gram(slab), slab)


def solution(mesh):
    placed = (P(("rows", "group"), None),)
    return jax.shard_map(
        local, mesh=mesh, in_specs=placed, out_specs=P(("rows", "group"), None), check_vma=False
    )
```
